32 devices in a mesh: row: 8 (over z, x), col: 4 (over y, core).
Axes of the slice: x: 2, y: 2, z: 4, core: 2. Of those that a mesh axis runs over, the one named last changes fastest.
Arguments:
- corner: bfloat16 [8, 4, 64, 64], P('row', 'col'), may hold values from -0.75 to 0.75
- top_edge: bfloat16 [8, 4, 64, 1024], P('row', 'col'), may hold values from -0.75 to 0.75
- left_edge: bfloat16 [8, 4, 64, 1024], P('row', 'col'), may hold values from -0.75 to 0.75
- site_tensor: bfloat16 [8, 4, 2, 4, 4, 4, 4], P('row', 'col'), may hold values from -1.3984375 to 1.3984375
- sketch: bfloat16 [8, 4, 64, 1024], P('row', 'col'), may hold values from -0.1875 to 0.1875
- grad_left: bfloat16 [8, 4, 64, 1024], P('row', 'col'), may hold values from -0.019897461 to 0.019897461
- grad_top: bfloat16 [8, 4, 64, 1024], P('row', 'col'), may hold values from -0.019897461 to 0.019897461
Outputs:
- corner_grad: bfloat16 [8, 4, 64, 64], P('row', 'col')
- top_grad: bfloat16 [8, 4, 64, 1024], P('row', 'col')
- left_grad: bfloat16 [8, 4, 64, 1024], P('row', 'col')
- site_grad: float32 [8, 4, 2, 4, 4, 4, 4], P('row', 'col')
The draws below stay inside these ranges and needn't reach their ends.
All inputs are finite; a program needn't handle non-finite values.
Results may differ from the reference program's by a relative error of at most 0.014.
Values may be sent and summed in bfloat16 or wider, within the bound.
A program may use at most 64 MiB of HBM per device.

```python
import jax
import jax.numpy as jnp
from jax import lax

CHI = 64
D = 4
PHYS = 2
DD = 16
NR = 8
NC = 4
N_ROW = 8
N_COL = 4


def levels(own_key, shape, pieces, low, top_value):
    def one(axis_at, shards_of):
        steps = jax.random.uniform(jax.random.fold_in(jax.random.fold_in(own_key, 6), axis_at), (shards_of,), jnp.float32, low / len(pieces), top_value / len(pieces))
        return jnp.repeat(jnp.exp(steps), shape[axis_at] // shards_of).reshape((-1,) + (1,) * (len(shape) - axis_at - 1))

    gain = one(*pieces[0])
    for cut in pieces[1:]:
        gain = gain * one(*cut)
    return gain


def normal_values(rng, dims, scale, reach, cuts=(), kind=jnp.bfloat16):
    entries = scale * jax.random.normal(rng, dims, jnp.float32)
    if cuts:
        entries = entries * levels(rng, dims, cuts, -0.22, 0.18)
    return jnp.clip(entries, -reach, reach).astype(kind)


def setup_inputs(seed: int = 0) -> dict:
    key_of = jax.random.split(jax.random.key(seed), 8)
    corner = normal_values(key_of[0], (NR, NC, CHI, CHI), CHI ** -0.5, 0.75, ((0, 8), (1, 4)))
    top_edge = normal_values(key_of[1], (NR, NC, CHI, DD * CHI), CHI ** -0.5, 0.75, ((0, 8), (1, 4)))
    left_edge = normal_values(key_of[2], (NR, NC, CHI, DD * CHI), CHI ** -0.5, 0.75, ((0, 8), (1, 4)))
    site_tensor = normal_values(key_of[3], (NR, NC, PHYS, D, D, D, D), 0.22, 1.3984375, ((0, 8), (1, 4)))
    sketch = normal_values(key_of[4], (NR, NC, CHI, DD * CHI), (DD * CHI) ** -0.5, 0.1875, ((0, 8), (1, 4)))
    grad_left = normal_values(key_of[5], (NR, NC, CHI, DD * CHI), 0.003, 0.019897461, ((0, 8), (1, 4)))
    grad_top = normal_values(key_of[6], (NR, NC, CHI, DD * CHI), 0.003, 0.019897461, ((0, 8), (1, 4)))
    return dict(corner=corner, top_edge=top_edge, left_edge=left_edge, site_tensor=site_tensor, sketch=sketch, grad_left=grad_left, grad_top=grad_top)


def contract(form, left_op, right_op):
    return jnp.einsum(form, left_op.astype(jnp.float32), right_op.astype(jnp.float32))


def mat_prod(left_op, right_op):
    return jnp.dot(left_op, right_op, preferred_element_type=jnp.float32)


def layers(corner_used, top_used, left_used, tensor_site):
    env_dim = corner_used.shape[0]
    bond_dim = tensor_site.shape[1]
    leg_dim = bond_dim * bond_dim
    top_mat = top_used
    first_prod = mat_prod(corner_used, top_mat).astype(jnp.bfloat16)
    left_three = left_used.reshape(env_dim, leg_dim, env_dim)
    second_prod = contract('lwm,lx->wmx', left_three, first_prod).astype(jnp.bfloat16)
    second_six = second_prod.reshape(bond_dim, bond_dim, env_dim, bond_dim, bond_dim, env_dim)
    ket_layer = contract('abmcet,pcavs->pbmevst', second_six, tensor_site).astype(jnp.bfloat16)
    return top_mat, first_prod, second_six, ket_layer


def forward_site(operands):
    corner_used, top_used, left_used, tensor_site, own_sketch, own_gleft, own_gtop = operands
    top_mat, first_prod, second_six, ket_layer = layers(corner_used, top_used, left_used, tensor_site)
    order_total = own_sketch.shape[1]
    quadrant = contract('pbmevst,pebxz->szmvxt', ket_layer, tensor_site).astype(jnp.bfloat16)
    quadrant = quadrant.reshape(order_total, order_total)
    sketched = mat_prod(own_sketch, quadrant.T).astype(jnp.bfloat16)
    downward = mat_prod(own_gleft, quadrant).astype(jnp.bfloat16)
    rightward = mat_prod(own_gtop, quadrant.T).astype(jnp.bfloat16)
    return sketched, downward, rightward


def backward_site(operands):
    corner_used, top_used, left_used, tensor_site, left_factor, right_factor = operands
    top_mat, first_prod, second_six, ket_layer = layers(corner_used, top_used, left_used, tensor_site)
    env_dim = corner_used.shape[0]
    bond_dim = tensor_site.shape[1]
    leg_dim = bond_dim * bond_dim
    grad_quad = jnp.dot(left_factor.T, right_factor, preferred_element_type=jnp.float32).astype(jnp.bfloat16)
    grad_quad = grad_quad.reshape(bond_dim, bond_dim, env_dim, bond_dim, bond_dim, env_dim)
    grad_ket = contract('szmvxt,pebxz->pbmevst', grad_quad, tensor_site).astype(jnp.bfloat16)
    bra_part = contract('pbmevst,szmvxt->pebxz', ket_layer, grad_quad)
    grad_second = contract('pbmevst,pcavs->abmcet', grad_ket, tensor_site).astype(jnp.bfloat16)
    ket_part = contract('abmcet,pbmevst->pcavs', second_six, grad_ket)
    grad_mat = grad_second.reshape(leg_dim, env_dim, leg_dim * env_dim)
    left_three = left_used.reshape(env_dim, leg_dim, env_dim)
    grad_first = contract('lwm,wmx->lx', left_three, grad_mat).astype(jnp.bfloat16)
    grad_lefted = contract('lx,wmx->lwm', first_prod, grad_mat).astype(jnp.bfloat16).reshape(left_used.shape)
    grad_topped = mat_prod(corner_used.T, grad_first).astype(jnp.bfloat16)
    grad_cornered = mat_prod(grad_first, top_mat.T).astype(jnp.bfloat16)
    return grad_cornered, grad_topped, grad_lefted, ket_part + bra_part


def flatten(tensor):
    return tensor.reshape((N_ROW * N_COL,) + tensor.shape[2:])


def unflatten(tensor):
    return tensor.reshape((N_ROW, N_COL) + tensor.shape[1:])


def reference(corner, top_edge, left_edge, site_tensor, sketch, grad_left, grad_top):
    corner_used = jnp.roll(corner, (1, 1), axis=(0, 1))
    top_used = jnp.roll(top_edge, 1, axis=0)
    left_used = jnp.roll(left_edge, 1, axis=1)
    used = (flatten(corner_used), flatten(top_used), flatten(left_used), flatten(site_tensor))
    sketched, downward, rightward = lax.map(forward_site, used + (flatten(sketch), flatten(grad_left), flatten(grad_top)))
    sketched = unflatten(sketched)
    downward = unflatten(downward)
    rightward = unflatten(rightward)
    sketch_below = jnp.roll(sketched, -1, axis=0)
    sketch_beside = jnp.roll(sketched, -1, axis=1)
    arrived = (jnp.roll(downward, 1, axis=0).astype(jnp.float32) + jnp.roll(rightward, 1, axis=1).astype(jnp.float32)).astype(jnp.bfloat16)
    left_factor = jnp.concatenate([grad_left, sketch_beside, arrived], axis=2)
    right_factor = jnp.concatenate([sketch_below, grad_top, sketch], axis=2)
    grad_cornered, grad_topped, grad_lefted, site_grad = lax.map(backward_site, used + (flatten(left_factor), flatten(right_factor)))
    corner_grad = jnp.roll(unflatten(grad_cornered), (-1, -1), axis=(0, 1))
    top_grad = jnp.roll(unflatten(grad_topped), -1, axis=0)
    left_grad = jnp.roll(unflatten(grad_lefted), -1, axis=1)
    return corner_grad, top_grad, left_grad, unflatten(site_grad)
```

```python
import functools

import jax
import jax.numpy as jnp
from jax import lax
from jax.experimental import pallas as pl
from jax.experimental.pallas import tpu as pltpu
from jax.sharding import PartitionSpec as P

MESH = pl.DeviceIdType.MESH
F32 = jnp.float32
BF16 = jnp.bfloat16


def mm(a, b):
    return lax.dot_general(a, b, (((1,), (0,)), ((), ())), preferred_element_type=F32)


def mm_nt(a, b):
    return lax.dot_general(a, b, (((1,), (1,)), ((), ())), preferred_element_type=F32)


def edge_rows(x, scr, legs, chi):
    half = chi // 2
    x = x.astype(F32)
    scr[...] = jnp.concatenate([x, pltpu.roll(x, legs * chi - half, 1)], axis=0).T
    parts = [scr[pl.ds(m, legs, stride=chi), :] for m in range(half)]
    return jnp.concatenate(parts, axis=0)


def edge_lanes(p, scr, legs, chi):
    half = chi // 2
    for m in range(half):
        scr[pl.ds(m, legs, stride=chi), :] = p[m * legs : (m + 1) * legs, :]
    x = scr[...].T
    low = lax.rem(lax.broadcasted_iota(jnp.int32, (chi, legs * chi), 1), chi) < half
    return jnp.where(low, x[:chi], pltpu.roll(x[chi:], half, 1))


def spread(x, dst, row, legs, chi):
    two = 2 * chi
    x = x.astype(F32)
    low = lax.broadcasted_iota(jnp.int32, (chi, two), 1) < chi
    for j in range(legs // 2):
        tile = x[:, j * two : (j + 1) * two]
        turned = pltpu.roll(tile, chi, 1)
        for odd, (lo, hi) in enumerate(((tile, turned), (turned, tile))):
            cols = slice((2 * j + odd) * two, (2 * j + odd + 1) * two)
            dst[row : row + chi, cols] = jnp.where(low, lo, 0.0).astype(BF16)
            dst[row + chi : row + two, cols] = jnp.where(low, 0.0, hi).astype(BF16)


def gather_diag(x, legs, chi):
    two = 2 * chi
    low = lax.broadcasted_iota(jnp.int32, (chi, two), 1) < chi
    out = []
    for j in range(legs // 2):
        even = x[:, 2 * j * two : (2 * j + 1) * two]
        odd = x[:, (2 * j + 1) * two : (2 * j + 2) * two]
        left = even[:chi] + pltpu.roll(even[chi:], chi, 1)
        right = pltpu.roll(odd[:chi], chi, 1) + odd[chi:]
        out.append(jnp.where(low, left, right))
    return jnp.concatenate(out, axis=1)


def to_blocks(x, legs, two):
    count = x.shape[0] // legs
    return jnp.concatenate(
        [
            jnp.concatenate(
                [x[m * legs : (m + 1) * legs, u * two : (u + 1) * two] for u in range(legs)], axis=0
            )
            for m in range(count)
        ],
        axis=1,
    )


def to_rows(b, legs, two):
    count = b.shape[1] // two
    return jnp.concatenate(
        [
            jnp.concatenate(
                [b[u * legs : (u + 1) * legs, m * two : (m + 1) * two] for u in range(legs)], axis=1
            )
            for m in range(count)
        ],
        axis=0,
    )


def picks(bond, which, across):
    legs = bond * bond
    full = legs * legs
    shape = (legs, full) if across else (full, legs)
    r = lax.broadcasted_iota(jnp.int32, shape, 1 if across else 0)
    key = lax.broadcasted_iota(jnp.int32, shape, 0 if across else 1)
    hi, lo = r // legs, lax.rem(r, legs)
    if which == 0:
        got = (hi // bond) * bond + lo // bond
    else:
        got = lax.rem(hi, bond) * bond + lax.rem(lo, bond)
    return jnp.where(got == key, 1.0, 0.0).astype(BF16)


def kernel(
    sizes,
    c_ref, u_ref, l_ref, t_ref, sk_ref, gl_ref, gt_ref,
    corner_out, top_out, left_out, site_out,
    lp_own, lp, top_in, corner_in,
    sk_p, sk_n, right_p, down_p,
    skr_in, skb_in, right_in, down_in,
    dtop, dcorner, dleft,
    dtop_in, dcorner_in, dleft_in,
    scr, fbd, rf, lf, a_ref, at_ref, layer,
    secb, qrows, dqb, dsrows,
    send, recv,
):
    chi, bond, phys, chunk = sizes
    legs = bond * bond
    two = 2 * chi
    half = chi // 2
    nr, nc = lax.axis_size("row"), lax.axis_size("col")
    r, c = lax.axis_index("row"), lax.axis_index("col")
    rn, rp = lax.rem(r + 1, nr), lax.rem(r + nr - 1, nr)
    cn, cp = lax.rem(c + 1, nc), lax.rem(c + nc - 1, nc)

    barrier = pltpu.get_barrier_semaphore()
    others = ((rn, c), (rp, c), (r, cn), (r, cp), (rn, cn), (rp, cp))
    for other in others:
        pl.semaphore_signal(barrier, inc=1, device_id=other, device_id_type=MESH)
    lp_own[...] = edge_rows(l_ref[...], scr, legs, chi).astype(BF16)
    pl.semaphore_wait(barrier, len(others))

    def put(n, src, dst, to):
        copy = pltpu.make_async_remote_copy(
            src_ref=src, dst_ref=dst, send_sem=send.at[n], recv_sem=recv.at[n],
            device_id=to, device_id_type=MESH,
        )
        copy.start()
        return copy

    top_copy = put(0, u_ref, top_in, (rn, c))
    corner_copy = put(1, c_ref, corner_in, (rn, cn))
    left_copy = put(2, lp_own, lp, (r, cn))

    for p in range(phys):
        site = t_ref[p * legs : (p + 1) * legs, :]
        for which in range(2):
            wide = mm(site, picks(bond, which, True)).astype(BF16)
            layer[p, which] = mm(picks(bond, which, False), wide).astype(BF16)
    double = sum(
        layer[p, 0].astype(F32) * layer[p, 1].astype(F32) for p in range(phys)
    )
    at_ref[...] = double.astype(BF16)
    a_ref[...] = double.T.astype(BF16)
    spread(gt_ref[...], rf, two, legs, chi)
    spread(sk_ref[...], rf, 2 * two, legs, chi)
    glp = edge_rows(gl_ref[...], scr, legs, chi)
    lf[:, :two] = glp.astype(BF16)
    glp_t = glp.T.astype(BF16)

    top_copy.wait()
    corner_copy.wait()
    first = mm(corner_in[...], top_in[...]).astype(BF16)
    spread(first, fbd, 0, legs, chi)
    left_copy.wait()

    rows_step = chunk * legs
    lanes_step = chunk * two
    steps = half // chunk

    @pl.loop(0, steps)
    def _(n):
        rows = pl.ds(pl.multiple_of(n * rows_step, rows_step), rows_step)
        lanes = pl.ds(pl.multiple_of(n * lanes_step, lanes_step), lanes_step)
        block = to_blocks(mm(lp[rows, :], fbd[...]).astype(BF16), legs, two)
        secb[:, lanes] = block
        qrows[rows, :] = to_rows(mm(a_ref[...], block).astype(BF16), legs, two)

    both = mm_nt(qrows[...], rf[two:, :]).astype(BF16)
    right_p[...] = both[:, :two]
    sk_p[...] = both[:, two:]
    skr_copy = put(3, sk_p, skr_in, (r, cp))
    right_copy = put(5, right_p, right_in, (r, cn))
    sk_n[...] = edge_lanes(both[:, two:].astype(F32), scr, legs, chi).astype(BF16)
    skb_copy = put(4, sk_n, skb_in, (rp, c))
    down = gather_diag(mm(glp_t, qrows[...]), legs, chi).astype(BF16)
    down_p[...] = edge_rows(down, scr, legs, chi).astype(BF16)
    down_copy = put(6, down_p, down_in, (rn, c))

    lp_t = lp[...].astype(F32).T.astype(BF16)
    skr_copy.wait()
    lf[:, two : 2 * two] = skr_in[...]
    skb_copy.wait()
    spread(skb_in[...], rf, 0, legs, chi)
    right_copy.wait()
    down_copy.wait()
    lf[:, 2 * two :] = (down_in[...].astype(F32) + right_in[...].astype(F32)).astype(BF16)

    @pl.loop(0, steps)
    def _(n):
        rows = pl.ds(pl.multiple_of(n * rows_step, rows_step), rows_step)
        lanes = pl.ds(pl.multiple_of(n * lanes_step, lanes_step), lanes_step)
        block = to_blocks(mm(lf[rows, :], rf[...]).astype(BF16), legs, two)
        dqb[:, lanes] = block
        dsrows[rows, :] = to_rows(mm(at_ref[...], block).astype(BF16), legs, two)

    dfirst = gather_diag(mm(lp_t, dsrows[...]), legs, chi).astype(BF16)
    dtop[...] = mm(corner_in[...].astype(F32).T.astype(BF16), dfirst).astype(BF16)
    dtop_copy = put(7, dtop, dtop_in, (rp, c))
    dcorner[...] = mm_nt(dfirst, top_in[...]).astype(BF16)
    dcorner_copy = put(8, dcorner, dcorner_in, (rp, cp))
    dleft[...] = edge_lanes(mm_nt(dsrows[...], fbd[...]), scr, legs, chi).astype(BF16)
    dleft_copy = put(9, dleft, dleft_in, (r, cp))

    ddouble = mm_nt(secb[...], dqb[...])
    for p in range(phys):
        total = None
        for which in range(2):
            part = (ddouble * layer[p, 1 - which].astype(F32)).astype(BF16)
            part = mm(picks(bond, which, True), part).astype(BF16)
            part = mm(part, picks(bond, which, False))
            total = part if total is None else total + part
        site_out[p * legs : (p + 1) * legs, :] = total

    dtop_copy.wait()
    top_out[...] = dtop_in[...]
    dcorner_copy.wait()
    corner_out[...] = dcorner_in[...]
    dleft_copy.wait()
    left_out[...] = dleft_in[...]


def local(corner, top_edge, left_edge, site_tensor, sketch, grad_left, grad_top):
    chi = corner.shape[2]
    phys, bond = site_tensor.shape[2:4]
    legs = bond * bond
    width = legs * chi
    two = 2 * chi
    rows = legs * chi // 2
    wide = legs * two
    full = legs * legs
    vm = lambda *shape: pltpu.VMEM(shape, BF16)
    edge = vm(chi, width)
    packed = vm(rows, two)
    tile = vm(chi, chi)
    spec = pl.BlockSpec(memory_space=pltpu.VMEM)
    outs = pl.pallas_call(
        functools.partial(kernel, (chi, bond, phys, 8)),
        out_shape=(
            jax.ShapeDtypeStruct((chi, chi), BF16),
            jax.ShapeDtypeStruct((chi, width), BF16),
            jax.ShapeDtypeStruct((chi, width), BF16),
            jax.ShapeDtypeStruct((phys * legs, legs), F32),
        ),
        in_specs=[spec] * 7,
        out_specs=(spec,) * 4,
        scratch_shapes=[
            packed, packed, edge, tile,
            packed, edge, packed, packed,
            packed, edge, packed, packed,
            edge, tile, edge,
            edge, tile, edge,
            pltpu.VMEM((width, two), F32),
            vm(two, wide), vm(3 * two, wide), vm(rows, 3 * two),
            vm(full, full), vm(full, full), vm(phys, 2, full, full),
            vm(full, rows * two // legs), vm(rows, wide), vm(full, rows * two // legs), vm(rows, wide),
            pltpu.SemaphoreType.DMA((10,)),
            pltpu.SemaphoreType.DMA((10,)),
        ],
        compiler_params=pltpu.CompilerParams(
            collective_id=0, has_side_effects=True, vmem_limit_bytes=48 * 1024 * 1024
        ),
    )(
        corner[0, 0], top_edge[0, 0], left_edge[0, 0],
        site_tensor.reshape(phys * legs, legs),
        sketch[0, 0], grad_left[0, 0], grad_top[0, 0],
    )
    return (
        outs[0][None, None], outs[1][None, None], outs[2][None, None],
        outs[3].reshape(site_tensor.shape),
    )


def solution(mesh):
    edges = P("row", "col", None, None)
    site = P("row", "col", None, None, None, None, None)
    return jax.shard_map(
        local, mesh=mesh,
        in_specs=(edges, edges, edges, site, edges, edges, edges),
        out_specs=(edges, edges, edges, site),
        check_vma=False,
    )
```

```python
import functools

import jax
import jax.numpy as jnp
from jax import lax
from jax.experimental import pallas as pl
from jax.experimental.pallas import tpu as pltpu
from jax.sharding import PartitionSpec as P

MESH = pl.DeviceIdType.MESH
F32 = jnp.float32
BF16 = jnp.bfloat16


def mm(a, b):
    return lax.dot_general(a, b, (((1,), (0,)), ((), ())), preferred_element_type=F32)


def mm_nt(a, b):
    return lax.dot_general(a, b, (((1,), (1,)), ((), ())), preferred_element_type=F32)


def edge_rows(x, scr, legs, chi):
    half = chi // 2
    x = x.astype(F32)
    scr[...] = jnp.concatenate([x, pltpu.roll(x, legs * chi - half, 1)], axis=0).T
    parts = [scr[pl.ds(m, legs, stride=chi), :] for m in range(half)]
    return jnp.concatenate(parts, axis=0)


def edge_lanes(p, scr, legs, chi):
    half = chi // 2
    for m in range(half):
        scr[pl.ds(m, legs, stride=chi), :] = p[m * legs : (m + 1) * legs, :]
    x = scr[...].T
    low = lax.rem(lax.broadcasted_iota(jnp.int32, (chi, legs * chi), 1), chi) < half
    return jnp.where(low, x[:chi], pltpu.roll(x[chi:], half, 1))


def spread(x, dst, row, legs, chi):
    two = 2 * chi
    x = x.astype(F32)
    low = lax.broadcasted_iota(jnp.int32, (chi, two), 1) < chi
    for j in range(legs // 2):
        tile = x[:, j * two : (j + 1) * two]
        turned = pltpu.roll(tile, chi, 1)
        for odd, (lo, hi) in enumerate(((tile, turned), (turned, tile))):
            cols = slice((2 * j + odd) * two, (2 * j + odd + 1) * two)
            dst[row : row + chi, cols] = jnp.where(low, lo, 0.0).astype(BF16)
            dst[row + chi : row + two, cols] = jnp.where(low, 0.0, hi).astype(BF16)


def gather_diag(x, legs, chi):
    two = 2 * chi
    low = lax.broadcasted_iota(jnp.int32, (chi, two), 1) < chi
    out = []
    for j in range(legs // 2):
        even = x[:, 2 * j * two : (2 * j + 1) * two]
        odd = x[:, (2 * j + 1) * two : (2 * j + 2) * two]
        left = even[:chi] + pltpu.roll(even[chi:], chi, 1)
        right = pltpu.roll(odd[:chi], chi, 1) + odd[chi:]
        out.append(jnp.where(low, left, right))
    return jnp.concatenate(out, axis=1)


def to_blocks(x, legs, two):
    count = x.shape[0] // legs
    return jnp.concatenate(
        [
            jnp.concatenate(
                [x[m * legs : (m + 1) * legs, u * two : (u + 1) * two] for u in range(legs)], axis=0
            )
            for m in range(count)
        ],
        axis=1,
    )


def to_rows(b, legs, two):
    count = b.shape[1] // two
    return jnp.concatenate(
        [
            jnp.concatenate(
                [b[u * legs : (u + 1) * legs, m * two : (m + 1) * two] for u in range(legs)], axis=1
            )
            for m in range(count)
        ],
        axis=0,
    )


def picks(bond, which, across):
    full = bond**4
    legs = bond * bond
    tall = bond**3
    shape = (tall, full) if across else (full, tall)
    r = lax.broadcasted_iota(jnp.int32, shape, 1 if across else 0)
    key = lax.broadcasted_iota(jnp.int32, shape, 0 if across else 1) // bond
    hi, lo = r // legs, lax.rem(r, legs)
    if which == 0:
        got = (hi // bond) * bond + lo // bond
    else:
        got = lax.rem(hi, bond) * bond + lax.rem(lo, bond)
    return jnp.where(got == key, 1.0, 0.0).astype(BF16)


def picks_last(bond, which, across):
    full = bond**4
    shape = (bond, full) if across else (full, bond)
    r = lax.broadcasted_iota(jnp.int32, shape, 1 if across else 0)
    key = lax.broadcasted_iota(jnp.int32, shape, 0 if across else 1)
    lo = lax.rem(r, bond * bond)
    got = lo // bond if which == 0 else lax.rem(lo, bond)
    return jnp.where(got == key, 1.0, 0.0).astype(BF16)


def same_v(bond, which):
    shape = (bond**3, bond**4)
    v = lax.rem(lax.broadcasted_iota(jnp.int32, shape, 0), bond)
    hi = lax.broadcasted_iota(jnp.int32, shape, 1) // (bond * bond)
    return v == (hi // bond if which == 0 else lax.rem(hi, bond))


def kernel(
    sizes,
    c_ref, u_ref, l_ref, t_ref, sk_ref, gl_ref, gt_ref,
    corner_out, top_out, left_out, site_out,
    lp_own, lp, top_in, corner_in,
    sk_p, right_p, down_p,
    skr_in, skb_in, right_in, down_in,
    dtop, dcorner, dleft,
    scr, fbd, rf, lf, a_ref, at_ref, layer,
    secb, qrows, dqb, dsrows,
    l_in, sk_in, gl_in, gt_in,
    send, recv, loads,
):
    chi, bond, phys, steps = sizes
    legs = bond * bond
    two = 2 * chi
    half = chi // 2
    nr, nc = lax.axis_size("row"), lax.axis_size("col")
    r, c = lax.axis_index("row"), lax.axis_index("col")
    rn, rp = lax.rem(r + 1, nr), lax.rem(r + nr - 1, nr)
    cn, cp = lax.rem(c + 1, nc), lax.rem(c + nc - 1, nc)

    barrier = pltpu.get_barrier_semaphore()
    others = ((rn, c), (rp, c), (r, cn), (r, cp), (rn, cn), (rp, cp))
    for other in others:
        pl.semaphore_signal(barrier, inc=1, device_id=other, device_id_type=MESH)
    fetch = [
        pltpu.make_async_copy(src, dst, loads.at[n])
        for n, (src, dst) in enumerate(
            ((l_ref, l_in), (gt_ref, gt_in), (sk_ref, sk_in), (gl_ref, gl_in))
        )
    ]
    for copy in fetch:
        copy.start()
    fetch[0].wait()
    lp_own[...] = edge_rows(l_in[...], scr, legs, chi).astype(BF16)
    pl.semaphore_wait(barrier, len(others))

    def put(n, src, dst, to):
        copy = pltpu.make_async_remote_copy(
            src_ref=src, dst_ref=dst, send_sem=send.at[n], recv_sem=recv.at[n],
            device_id=to, device_id_type=MESH,
        )
        copy.start()
        return copy

    top_copy = put(0, u_ref, top_in, (rn, c))
    corner_copy = put(1, c_ref, corner_in, (rn, cn))
    left_copy = put(2, lp_own, lp, (r, cn))

    for p in range(phys):
        site = jnp.concatenate(
            [
                t_ref[0, 0, p, u, w].astype(F32)
                for u in range(bond)
                for w in range(bond)
            ],
            axis=0,
        ).astype(BF16)
        for which in range(2):
            wide = mm(site, picks_last(bond, which, True))
            wide = jnp.where(same_v(bond, which), wide, 0.0).astype(BF16)
            layer[p, which] = mm(picks(bond, which, False), wide).astype(BF16)
    double = sum(
        layer[p, 0].astype(F32) * layer[p, 1].astype(F32) for p in range(phys)
    )
    at_ref[...] = double.astype(BF16)
    a_ref[...] = double.T.astype(BF16)
    for copy in fetch[1:]:
        copy.wait()
    spread(gt_in[...], rf, two, legs, chi)
    spread(sk_in[...], rf, 2 * two, legs, chi)
    glp = edge_rows(gl_in[...], scr, legs, chi)
    lf[:, :two] = glp.astype(BF16)
    glp_t = glp.T.astype(BF16)

    top_copy.wait()
    corner_copy.wait()
    first = mm(corner_in[...], top_in[...]).astype(BF16)
    spread(first, fbd, 0, legs, chi)
    left_copy.wait()

    rows_step = half * legs // steps
    lanes_step = half * two // steps
    parts = [
        (slice(n * rows_step, (n + 1) * rows_step), slice(n * lanes_step, (n + 1) * lanes_step))
        for n in range(steps)
    ]

    skb_copies, skr_copies, right_copies = [], [], []
    for n, (rows, lanes) in enumerate(parts):
        block = to_blocks(mm(lp[rows, :], fbd[...]).astype(BF16), legs, two)
        secb[:, lanes] = block
        quad = to_rows(mm(a_ref[...], block).astype(BF16), legs, two)
        qrows[rows, :] = quad
        both = mm_nt(quad, rf[two:, :]).astype(BF16)
        sk_p[rows, :] = both[:, two:]
        right_p[rows, :] = both[:, :two]
        at = 6 + 3 * n
        skb_copies.append(put(at, sk_p.at[rows], skb_in.at[rows], (rp, c)))
        skr_copies.append(put(at + 1, sk_p.at[rows], skr_in.at[rows], (r, cp)))
        right_copies.append(put(at + 2, right_p.at[rows], right_in.at[rows], (r, cn)))

    down = gather_diag(mm(glp_t, qrows[...]), legs, chi).astype(BF16)
    down_p[...] = edge_rows(down, scr, legs, chi).astype(BF16)
    down_copy = put(3, down_p, down_in, (rn, c))

    lp_t = lp[...].astype(F32).T.astype(BF16)
    for copy in skr_copies:
        copy.wait()
    lf[:, two : 2 * two] = skr_in[...]
    for copy in skb_copies:
        copy.wait()
    spread(edge_lanes(skb_in[...].astype(F32), scr, legs, chi), rf, 0, legs, chi)
    for copy in right_copies:
        copy.wait()
    down_copy.wait()
    lf[:, 2 * two :] = (down_in[...].astype(F32) + right_in[...].astype(F32)).astype(BF16)

    for rows, lanes in parts:
        block = to_blocks(mm(lf[rows, :], rf[...]).astype(BF16), legs, two)
        dqb[:, lanes] = block
        dsrows[rows, :] = to_rows(mm(at_ref[...], block).astype(BF16), legs, two)

    dfirst = gather_diag(mm(lp_t, dsrows[...]), legs, chi).astype(BF16)
    dtop[...] = mm(corner_in[...].astype(F32).T.astype(BF16), dfirst).astype(BF16)
    dtop_copy = put(4, dtop, top_out, (rp, c))
    dcorner[...] = mm_nt(dfirst, top_in[...]).astype(BF16)
    dcorner_copy = put(5, dcorner, corner_out, (rp, cp))
    dleft[...] = edge_lanes(mm_nt(dsrows[...], fbd[...]), scr, legs, chi).astype(BF16)
    dleft_copy = put(6 + 3 * steps, dleft, left_out, (r, cp))

    ddouble = mm_nt(secb[...], dqb[...])
    for p in range(phys):
        total = None
        for which in range(2):
            part = (ddouble * layer[p, 1 - which].astype(F32)).astype(BF16)
            part = mm(picks(bond, which, True), part)
            part = jnp.where(same_v(bond, which), part, 0.0).astype(BF16)
            part = mm(part, picks_last(bond, which, False))
            total = part if total is None else total + part
        for u in range(bond):
            for w in range(bond):
                at = (u * bond + w) * bond
                site_out[0, 0, p, u, w] = total[at : at + bond, :]

    dtop_copy.wait()
    dcorner_copy.wait()
    dleft_copy.wait()


def local(corner, top_edge, left_edge, site_tensor, sketch, grad_left, grad_top):
    chi = corner.shape[2]
    phys, bond = site_tensor.shape[2:4]
    legs = bond * bond
    width = legs * chi
    steps = 2
    two = 2 * chi
    rows = legs * chi // 2
    wide = legs * two
    full = legs * legs
    vm = lambda *shape: pltpu.VMEM(shape, BF16)
    edge = vm(chi, width)
    packed = vm(rows, two)
    tile = vm(chi, chi)
    spec = pl.BlockSpec(memory_space=pltpu.VMEM)
    hbm = pl.BlockSpec(memory_space=pltpu.HBM)
    outs = pl.pallas_call(
        functools.partial(kernel, (chi, bond, phys, steps)),
        out_shape=(
            jax.ShapeDtypeStruct((chi, chi), BF16),
            jax.ShapeDtypeStruct((chi, width), BF16),
            jax.ShapeDtypeStruct((chi, width), BF16),
            jax.ShapeDtypeStruct(site_tensor.shape, F32),
        ),
        in_specs=[hbm, hbm, hbm, spec, hbm, hbm, hbm],
        out_specs=(spec,) * 4,
        scratch_shapes=[
            packed, packed, edge, tile,
            packed, packed, packed,
            packed, packed, packed, packed,
            edge, tile, edge,
            pltpu.VMEM((width, two), F32),
            vm(two, wide), vm(3 * two, wide), vm(rows, 3 * two),
            vm(full, full), vm(full, full), vm(phys, 2, full, full),
            vm(full, rows * two // legs), vm(rows, wide), vm(full, rows * two // legs), vm(rows, wide),
            edge, edge, edge, edge,
            pltpu.SemaphoreType.DMA((7 + 3 * steps,)),
            pltpu.SemaphoreType.DMA((7 + 3 * steps,)),
            pltpu.SemaphoreType.DMA((4,)),
        ],
        compiler_params=pltpu.CompilerParams(
            collective_id=0, has_side_effects=True, vmem_limit_bytes=60 * 1024 * 1024
        ),
    )(
        corner[0, 0], top_edge[0, 0], left_edge[0, 0],
        site_tensor,
        sketch[0, 0], grad_left[0, 0], grad_top[0, 0],
    )
    return (
        outs[0][None, None], outs[1][None, None], outs[2][None, None],
        outs[3],
    )


def solution(mesh):
    edges = P("row", "col", None, None)
    site = P("row", "col", None, None, None, None, None)
    return jax.shard_map(
        local, mesh=mesh,
        in_specs=(edges, edges, edges, site, edges, edges, edges),
        out_specs=(edges, edges, edges, site),
        check_vma=False,
    )
```
